512 devices in a mesh: grp: 2 (over core), seq: 128 (over z_hi, x, y), dp: 2 (over z_lo).
Axes of the slice: x: 4, y: 8, z: 8 (z_hi: 4, z_lo: 2; z = z_hi * 2 + z_lo), core: 2. Of those that a mesh axis runs over, the one named last changes fastest.
Arguments:
- qkv: bfloat16 [2, 3, 2, 22528, 1536], P('grp', None, 'dp', 'seq'), may hold values from -4.5 to 4.5
- cotangent: bfloat16 [2, 2, 22528, 1536], P('grp', 'dp', 'seq'), may hold values from -4 to 4
- gate: float32 [1536], replicated, may hold values from 0.5 to 2
- tile_map: int32 [2, 32, 704], P('dp'), may hold values from 0 to 703, as said below
- text_count: int32 [2, 32], P('dp'), may hold values from 1 to 128
Outputs:
- blended: bfloat16 [2, 2, 22528, 1536], P('grp', 'dp', 'seq')
- input_grads: bfloat16 [2, 3, 2, 22528, 1536], P('grp', None, 'dp', 'seq')
- gate_grad: float32 [1536], replicated
The draws below stay inside these ranges and needn't reach their ends.
Inputs may be any that keep to these rules, and one draw needn't show every extreme that they name: `tile_map`: each row keeps positions below 128 in place and lists the image tokens tile by tile, 4 x 4 tokens a tile, of an image 24 tokens a side; every row is a permutation.
All inputs are finite; a program needn't handle non-finite values.
Results may differ from the reference program's by a relative error of at most 0.0062.
Values may be sent and summed in bfloat16 or wider, within the bound.
A program may use at most 64 MiB of HBM per device.

```python
import math
import jax
import jax.numpy as jnp
from jax import lax

HEADS = 12
HD = 128
TILE = 4
TXT = 128
SIDE = 24
C = 1536
IMG = 576
L = 704
SEQS = 32
N_DP = 2


def draw_qkv(key, part):
    key = jax.random.fold_in(key, 7)
    extent = (2, 3, N_DP, SEQS, L, C)
    noise_key = jax.random.fold_in(key, 0)
    scales = jnp.array([1.2, 1.2, 1.5], jnp.float32).reshape(1, 3, 1, 1, 1, 1)
    drawn = jax.random.truncated_normal(noise_key, -3.0, 3.0, extent, jnp.float32) * scales
    return drawn.reshape(2, 3, N_DP, SEQS * L, C).astype(jnp.bfloat16)


def draw_tile_map(key, part):
    key = jax.random.fold_in(key, 19)
    across = SIDE // TILE
    tile_count = across * across
    key_list = jax.random.split(key, N_DP * SEQS)
    orders = jax.vmap(lambda subkey: jax.random.permutation(subkey, tile_count))(key_list)
    inside = jnp.arange(TILE * TILE, dtype=jnp.int32)
    tile_row = inside // TILE
    tile_col = inside % TILE
    chosen = orders[:, :, None].astype(jnp.int32)
    token_ids = TXT + (chosen // across * TILE + tile_row[None, None, :]) * SIDE + chosen % across * TILE + tile_col[None, None, :]
    image_part = token_ids.reshape(N_DP * SEQS, IMG)
    text_part = jnp.broadcast_to(jnp.arange(TXT, dtype=jnp.int32)[None, :], (N_DP * SEQS, TXT))
    return jnp.concatenate([text_part, image_part], axis=1).reshape(N_DP, SEQS, L).astype(jnp.int32)


def draw_text_count(key, part):
    key = jax.random.fold_in(key, 23)
    draw_key, forced_key = jax.random.split(key)
    counts = jax.random.randint(draw_key, (N_DP * SEQS,), 1, TXT + 1)
    forced = jax.random.randint(forced_key, (), 0, N_DP * SEQS)
    counts = counts.at[forced].set(TXT)
    return counts.reshape(N_DP, SEQS).astype(jnp.int32)


def levels(own_key, shape, pieces, low, largest):
    def one(dim, shards_of):
        draws = jax.random.uniform(jax.random.fold_in(jax.random.fold_in(own_key, 6), dim), (shards_of,), jnp.float32, low / len(pieces), largest / len(pieces))
        return jnp.repeat(jnp.exp(draws), shape[dim] // shards_of).reshape((-1,) + (1,) * (len(shape) - dim - 1))

    level = one(*pieces[0])
    for cut in pieces[1:]:
        level = level * one(*cut)
    return level


def bell_draw(stream_key, shape, spread, bound, pieces=(), held_as=jnp.bfloat16):
    values = spread * jax.random.normal(stream_key, shape, jnp.float32)
    if pieces:
        values = values * levels(stream_key, shape, pieces, -0.22, 0.18)
    return jnp.clip(values, -bound, bound).astype(held_as)


def setup_inputs(seed: int = 0) -> dict:
    seeds = jax.random.split(jax.random.key(seed), 6)
    return {
        "qkv": draw_qkv(jax.random.fold_in(seeds[5], 71), 0),
        "cotangent": bell_draw(seeds[1], (2, N_DP, SEQS * L, C), 1.0, 4.0, ((0, 2), (1, 2), (2, 128))),
        "gate": jnp.clip(jnp.exp(jax.random.uniform(seeds[2], (C,), jnp.float32, math.log(0.5), math.log(2.0))), 0.5, 2.0),
        "tile_map": draw_tile_map(jax.random.fold_in(seeds[5], 71), 0),
        "text_count": draw_text_count(jax.random.fold_in(seeds[5], 71), 0),
    }


def attend(queries, keys_in, values, out_grad, usable):
    score_scale = 1.0 / math.sqrt(HD)
    query_f = queries.astype(jnp.float32).reshape(L, HEADS, HD)
    key_f = keys_in.astype(jnp.float32).reshape(L, HEADS, HD)
    value_f = values.astype(jnp.float32).reshape(L, HEADS, HD)
    grad_f = out_grad.astype(jnp.float32).reshape(L, HEADS, HD)
    scores = jnp.einsum('qhd,khd->hqk', query_f, key_f) * score_scale
    scores = jnp.where(usable[None, None, :], scores, -jnp.inf)
    attn_probs = jax.nn.softmax(scores, axis=-1)
    probs_low = lax.optimization_barrier(attn_probs.astype(jnp.bfloat16)).astype(jnp.float32)
    output = jnp.einsum('hqk,khd->qhd', probs_low, value_f)
    grad_probs = jnp.einsum('qhd,khd->hqk', grad_f, value_f)
    centre = lax.optimization_barrier(jnp.sum(attn_probs * grad_probs, axis=-1, keepdims=True))
    shifted = lax.optimization_barrier((attn_probs * (grad_probs - centre)).astype(jnp.bfloat16)).astype(jnp.float32)
    query_grad = jnp.einsum('hqk,khd->qhd', shifted, key_f) * score_scale
    key_grad = jnp.einsum('hqk,qhd->khd', shifted, query_f) * score_scale
    value_grad = jnp.einsum('hqk,qhd->khd', probs_low, grad_f)
    return (output.reshape(L, C), query_grad.reshape(L, C), key_grad.reshape(L, C), value_grad.reshape(L, C))

def reference(qkv, cotangent, gate, tile_map, text_count):
    total = N_DP * SEQS
    stacked = qkv.reshape(2, 3, total, L, C).transpose(2, 0, 1, 3, 4)
    upstream = cotangent.reshape(2, total, L, C).transpose(1, 0, 2, 3)
    orders = tile_map.reshape(total, L)
    counts = text_count.reshape(total)
    places = jnp.arange(L, dtype=jnp.int32)

    def one_sequence(items):
        inputs, grads_in, ordering, counted = items
        usable = (places >= TXT) | (places < counted)
        back_grad = jnp.take(grads_in[1], ordering, axis=0)
        control_grad = (grads_in[0].astype(jnp.float32) + gate[None, :] * back_grad.astype(jnp.float32)).astype(jnp.bfloat16)
        out_c, query_c, key_c, value_c = attend(inputs[0, 0], inputs[0, 1], inputs[0, 2], control_grad, usable)
        out_m, query_m, key_m, value_m = attend(inputs[1, 0], inputs[1, 1], inputs[1, 2], grads_in[1], usable)
        attn_c = out_c.astype(jnp.bfloat16)
        attn_m = out_m.astype(jnp.bfloat16)
        control_res = (gate[None, :] * attn_c.astype(jnp.float32)).astype(jnp.bfloat16)
        placed = jnp.zeros_like(control_res).at[ordering].set(control_res)
        base_out = (attn_m.astype(jnp.float32) + placed.astype(jnp.float32)).astype(jnp.bfloat16)
        blended_seq = jnp.stack([attn_c, base_out])
        grads_seq = jnp.stack([jnp.stack([query_c, key_c, value_c]), jnp.stack([query_m, key_m, value_m])]).astype(jnp.bfloat16)
        gate_term = lax.optimization_barrier(jnp.sum(attn_c.astype(jnp.float32) * back_grad.astype(jnp.float32), axis=0))
        return (blended_seq, grads_seq, gate_term)
    blended_all, grads_all, gate_terms = lax.map(one_sequence, (stacked, upstream, orders, counts))
    blended = blended_all.transpose(1, 0, 2, 3).reshape(2, N_DP, SEQS * L, C)
    input_grads = grads_all.transpose(1, 2, 0, 3, 4).reshape(2, 3, N_DP, SEQS * L, C)
    gate_grad = lax.optimization_barrier(jnp.sum(gate_terms, axis=0))
    return (blended, input_grads, gate_grad)
```

```python
import functools
import math

import jax
import jax.numpy as jnp
from jax import lax
from jax.experimental import pallas as pl
from jax.experimental.pallas import tpu as pltpu
from jax.sharding import PartitionSpec as P

HD = 128
GROUP = 4
TXT = 128
SCALE = 1.0 / math.sqrt(HD)
EXP2_SCALE = SCALE * math.log2(math.e)
MESH = pl.DeviceIdType.MESH
BF16 = jnp.bfloat16
F32 = jnp.float32


def flip(index, bit):
    unit = 1 << bit
    return index + unit - 2 * unit * lax.rem(lax.div(index, unit), 2)


def contract(left, right, left_dim, right_dim):
    return lax.dot_general(
        left, right, (((left_dim,), (right_dim,)), ((), ())), preferred_element_type=F32
    )


def kernel(
    heads,
    seq_bits,
    dp_size,
    qkv,
    cot,
    gate,
    tile_map,
    text_count,
    blended,
    grads,
    gate_grad,
    held,
    made,
    back_out,
    back_in,
    res_out,
    res_in,
    perm,
    perm_t,
    sums,
    sums_in,
    shares,
    in_send,
    in_recv,
    out_send,
    out_recv,
    back_sems,
    res_sems,
    sum_send,
    sum_recv,
    share_send,
    share_recv,
):
    core = lax.axis_index("grp")
    position = lax.axis_index("seq")
    member = lax.rem(position, GROUP)
    sequence = lax.div(position, GROUP)
    base = position - member
    rows = qkv.shape[3]
    length = rows * GROUP
    partners = [member, flip(member, 0), flip(member, 1), 3 - member]
    other_core = {"grp": 1 - core}
    steps = [other_core]
    if dp_size == 2:
        steps.append({"dp": 1 - lax.axis_index("dp")})
    steps += [{"seq": flip(position, bit)} for bit in reversed(range(2, seq_bits))]

    def rows_of(which):
        return pl.ds(pl.multiple_of(which * rows, 16), rows)

    def columns_of(which, head):
        return pl.ds(pl.multiple_of((which * heads + head) * HD, HD), HD)

    def in_pair(head, k):
        pairs = []
        theirs = columns_of(partners[k], head)
        mine = rows_of(member)
        for t, (src, dst) in enumerate(
            (
                (qkv.at[0, :, 0, :, theirs], held.at[head, pl.ds(0, 3), mine, :]),
                (cot.at[0, 0, :, theirs], held.at[head, 3, mine, :]),
            )
        ):
            if k == 0:
                pairs.append(pltpu.make_async_copy(src, dst, in_recv.at[head, k, t]))
            else:
                pairs.append(
                    pltpu.make_async_remote_copy(
                        src_ref=src,
                        dst_ref=dst,
                        send_sem=in_send.at[head, k, t],
                        recv_sem=in_recv.at[head, k, t],
                        device_id={"seq": base + partners[k]},
                        device_id_type=MESH,
                    )
                )
        return pairs

    def in_arrival(head, k):
        theirs = rows_of(partners[k])
        pairs = []
        for t, dst in enumerate(
            (held.at[head, pl.ds(0, 3), theirs, :], held.at[head, 3, theirs, :])
        ):
            pairs.append(
                pltpu.make_async_remote_copy(
                    src_ref=dst,
                    dst_ref=dst,
                    send_sem=in_send.at[head, k, t],
                    recv_sem=in_recv.at[head, k, t],
                    device_id={"seq": base + partners[k]},
                    device_id_type=MESH,
                )
            )
        return pairs

    def out_pair(head, k, t):
        theirs = rows_of(partners[k])
        mine = columns_of(member, head)
        if t == 0:
            src, dst = made.at[head, 0, theirs, :], blended.at[0, 0, :, mine]
        else:
            src, dst = made.at[head, pl.ds(1, 3), theirs, :], grads.at[0, :, 0, :, mine]
        if k == 0:
            return pltpu.make_async_copy(src, dst, out_recv.at[head, k, t])
        return pltpu.make_async_remote_copy(
            src_ref=src,
            dst_ref=dst,
            send_sem=out_send.at[head, k, t],
            recv_sem=out_recv.at[head, k, t],
            device_id={"seq": base + partners[k]},
            device_id_type=MESH,
        )

    def out_arrival(head, k, t):
        theirs = columns_of(partners[k], head)
        if t == 0:
            dst = blended.at[0, 0, :, theirs]
        else:
            dst = grads.at[0, :, 0, :, theirs]
        return pltpu.make_async_remote_copy(
            src_ref=dst,
            dst_ref=dst,
            send_sem=out_send.at[head, k, t],
            recv_sem=out_recv.at[head, k, t],
            device_id={"seq": base + partners[k]},
            device_id_type=MESH,
        )

    def back_copy(head):
        return pltpu.make_async_remote_copy(
            src_ref=back_out.at[head],
            dst_ref=back_in.at[head],
            send_sem=back_sems.at[head, 0],
            recv_sem=back_sems.at[head, 1],
            device_id=other_core,
            device_id_type=MESH,
        )

    def res_copy(head):
        return pltpu.make_async_remote_copy(
            src_ref=res_out.at[head],
            dst_ref=res_in.at[head],
            send_sem=res_sems.at[head, 0],
            recv_sem=res_sems.at[head, 1],
            device_id=other_core,
            device_id_type=MESH,
        )

    barrier = pltpu.get_barrier_semaphore()
    peers = [{"seq": base + partners[k]} for k in (1, 2, 3)] + steps
    for peer in peers:
        pl.semaphore_signal(barrier, inc=1, device_id=peer, device_id_type=MESH)
    pl.semaphore_wait(barrier, len(peers))

    for head in range(heads):
        for k in (2, 3, 1, 0):
            for copy in in_pair(head, k):
                copy.start()

    sums[0] = jnp.zeros(sums.shape[1:], F32)

    @pl.when(core == 1)
    def _():
        order = tile_map[0, pl.ds(sequence, 1), :].astype(F32)
        down = lax.broadcasted_iota(jnp.int32, (length, length), 0).astype(F32)
        perm_t[...] = jnp.where(down == order, 1.0, 0.0).astype(BF16)
        order_down = jnp.transpose(jnp.broadcast_to(order, (HD, length)))
        for start in range(0, length, HD):
            width = min(HD, length - start)
            across = lax.broadcasted_iota(jnp.int32, (length, width), 1).astype(F32) + start
            perm[:, start : start + width] = jnp.where(
                order_down[:, :width] == across, 1.0, 0.0
            ).astype(BF16)

    counted = text_count[0, sequence]

    def one_head(head, carry):
        for k in (0, 1, 2, 3):
            for copy in in_pair(head, k) if k == 0 else in_arrival(head, k):
                if k == 0:
                    copy.wait()
                else:
                    copy.wait_recv()

        gains = gate[pl.ds(member * heads + head, 1), :]

        @pl.when(core == 1)
        def _():
            back_out[head] = contract(perm[...], held[head, 3], 1, 0).astype(BF16)
            back_copy(head).start()

        @pl.when(core == 0)
        def _():
            back_copy(head).wait_recv()
            held[head, 3] = (
                held[head, 3].astype(F32) + gains * back_in[head].astype(F32)
            ).astype(BF16)

        keys = held[head, 1]
        values = held[head, 2]
        key_sum = None
        for start in range(0, length, 256):
            width = min(256, length - start)
            span = pl.ds(start, width)
            queries = held[head, 0, span, :]
            grad = held[head, 3, span, :]
            scores = contract(keys, queries, 1, 1)
            text = lax.broadcasted_iota(jnp.int32, (TXT, width), 0) < counted
            scores = jnp.concatenate(
                [jnp.where(text, scores[:TXT], -jnp.inf), scores[TXT:]], axis=0
            )
            top = jnp.max(scores, axis=0, keepdims=True)
            grown = jnp.exp2((scores - top) * EXP2_SCALE)
            probs = grown * (1.0 / jnp.sum(grown, axis=0, keepdims=True))
            probs_low = probs.astype(BF16)
            made[head, 0, span, :] = jnp.transpose(contract(values, probs_low, 0, 0)).astype(BF16)
            grad_probs = contract(values, grad, 1, 1)
            centre = jnp.sum(probs * grad_probs, axis=0, keepdims=True)
            shifted = (probs * (grad_probs - centre)).astype(BF16)
            made[head, 1, span, :] = (
                jnp.transpose(contract(keys, shifted, 0, 0)) * SCALE
            ).astype(BF16)
            key_part = contract(shifted, queries, 1, 0)
            value_part = contract(probs_low, grad, 1, 0)
            key_sum = key_part if key_sum is None else key_sum + key_part
            value_sum = value_part if start == 0 else value_sum + value_part
        made[head, 2] = (key_sum * SCALE).astype(BF16)
        made[head, 3] = value_sum.astype(BF16)
        for k in (2, 3, 1, 0):
            out_pair(head, k, 1).start()

        @pl.when(core == 0)
        def _():
            own = made[head, 0].astype(F32)
            res_out[head] = (gains * own).astype(BF16)
            res_copy(head).start()
            sums[0, pl.ds(head, 1), :] = jnp.sum(
                own * back_in[head].astype(F32), axis=0, keepdims=True
            )

        @pl.when(core == 1)
        def _():
            res_copy(head).wait_recv()
            placed = contract(perm_t[...], res_in[head], 1, 0)
            made[head, 0] = (made[head, 0].astype(F32) + placed).astype(BF16)

        for k in (2, 3, 1, 0):
            out_pair(head, k, 0).start()
        return carry

    lax.fori_loop(0, heads, one_head, 0)

    for step, peer in enumerate(steps):
        copy = pltpu.make_async_remote_copy(
            src_ref=sums.at[step],
            dst_ref=sums_in.at[step],
            send_sem=sum_send.at[step],
            recv_sem=sum_recv.at[step],
            device_id=peer,
            device_id_type=MESH,
        )
        copy.start()
        copy.wait()
        sums[step + 1] = sums[step] + sums_in[step]
    last = sums.at[len(steps)]

    def share_copy(k, slot):
        return pltpu.make_async_remote_copy(
            src_ref=last,
            dst_ref=shares.at[slot],
            send_sem=share_send.at[k],
            recv_sem=share_recv.at[k],
            device_id={"seq": base + partners[k]},
            device_id_type=MESH,
        )

    for k in (2, 3, 1):
        share_copy(k, member).start()
    shares[member] = last[...]
    for k in (1, 2, 3):
        share_copy(k, partners[k]).wait_recv()
    for k in (1, 2, 3):
        share_copy(k, member).wait_send()
    for which in range(GROUP):
        gate_grad[which * heads : (which + 1) * heads, :] = shares[which, :heads, :]

    def finish(head, carry):
        for k in (1, 2, 3):
            for copy in in_pair(head, k):
                copy.wait_send()
        for t in (0, 1):
            out_pair(head, 0, t).wait()
            for k in (1, 2, 3):
                out_pair(head, k, t).wait_send()
                out_arrival(head, k, t).wait_recv()

        @pl.when(core == 0)
        def _():
            res_copy(head).wait_send()

        @pl.when(core == 1)
        def _():
            back_copy(head).wait_send()

        return carry

    lax.fori_loop(0, heads, finish, 0)


def per_device(mesh, qkv, cotangent, gate, tile_map, text_count):
    rows, channels = qkv.shape[3:]
    length = rows * GROUP
    heads = channels // HD // GROUP
    seq_bits = mesh.shape["seq"].bit_length() - 1
    dp_size = mesh.shape["dp"]
    step_count = 1 + (dp_size == 2) + seq_bits - 2
    vmem = pl.BlockSpec(memory_space=pltpu.VMEM)
    any_space = pl.BlockSpec(memory_space=pl.ANY)
    dma = pltpu.SemaphoreType.DMA
    blended, grads, gate_grad = pl.pallas_call(
        functools.partial(kernel, heads, seq_bits, dp_size),
        out_shape=(
            jax.ShapeDtypeStruct(cotangent.shape, BF16),
            jax.ShapeDtypeStruct(qkv.shape, BF16),
            jax.ShapeDtypeStruct((channels // HD, HD), F32),
        ),
        in_specs=[
            any_space,
            any_space,
            vmem,
            vmem,
            pl.BlockSpec(memory_space=pltpu.SMEM),
        ],
        out_specs=(any_space, any_space, vmem),
        scratch_shapes=[
            pltpu.VMEM((heads, 4, length, HD), BF16),
            pltpu.VMEM((heads, 4, length, HD), BF16),
            pltpu.VMEM((heads, length, HD), BF16),
            pltpu.VMEM((heads, length, HD), BF16),
            pltpu.VMEM((heads, length, HD), BF16),
            pltpu.VMEM((heads, length, HD), BF16),
            pltpu.VMEM((length, length), BF16),
            pltpu.VMEM((length, length), BF16),
            pltpu.VMEM((step_count + 1, 8, HD), F32),
            pltpu.VMEM((step_count, 8, HD), F32),
            pltpu.VMEM((GROUP, 8, HD), F32),
            dma((heads, GROUP, 2)),
            dma((heads, GROUP, 2)),
            dma((heads, GROUP, 2)),
            dma((heads, GROUP, 2)),
            dma((heads, 2)),
            dma((heads, 2)),
            dma((step_count,)),
            dma((step_count,)),
            dma((GROUP,)),
            dma((GROUP,)),
        ],
        compiler_params=pltpu.CompilerParams(
            collective_id=0, has_side_effects=True, vmem_limit_bytes=48 * 1024 * 1024
        ),
    )(qkv, cotangent, gate.reshape(channels // HD, HD), tile_map, text_count)
    return blended, grads, gate_grad.reshape(channels)


def solution(mesh):
    placed = (
        P("grp", None, "dp", "seq", None),
        P("grp", "dp", "seq", None),
        P(),
        P("dp", None, None),
        P("dp", None),
    )
    return jax.shard_map(
        functools.partial(per_device, mesh),
        mesh=mesh,
        in_specs=placed,
        out_specs=(P("grp", "dp", "seq", None), P("grp", None, "dp", "seq", None), P()),
        check_vma=False,
    )
```

```python
import functools
import math

import jax
import jax.numpy as jnp
from jax import lax
from jax.experimental import pallas as pl
from jax.experimental.pallas import tpu as pltpu
from jax.sharding import PartitionSpec as P

HD = 128
GROUP = 4
TXT = 128
BLOCK = 704
SCALE = 1.0 / math.sqrt(HD)
EXP2_SCALE = SCALE * math.log2(math.e)
MESH = pl.DeviceIdType.MESH
BF16 = jnp.bfloat16
F32 = jnp.float32


def flip(index, bit):
    unit = 1 << bit
    return index + unit - 2 * unit * lax.rem(lax.div(index, unit), 2)


def contract(left, right, left_dim, right_dim):
    return lax.dot_general(
        left, right, (((left_dim,), (right_dim,)), ((), ())), preferred_element_type=F32
    )


def kernel(
    heads,
    sizes,
    qkv,
    cot,
    gate,
    tile_map,
    text_count,
    blended,
    grads,
    gate_grad,
    held,
    made,
    back_out,
    back_in,
    res_out,
    res_in,
    perm,
    perm_t,
    probs_all,
    probs_low_all,
    order_all,
    gains_all,
    counts,
    partial,
    z_slots,
    x_slots,
    y_slots,
    total,
    in_send,
    in_recv,
    out_send,
    out_recv,
    back_sems,
    res_sems,
    round_send,
    round_recv,
    total_sems,
    small_sems,
):
    z_size, dp_size, x_size, y_size = sizes
    core = lax.axis_index("grp")
    position = lax.axis_index("seq")
    sample = lax.axis_index("dp")
    member = lax.rem(position, GROUP)
    sequence = lax.div(position, GROUP)
    base = position - member
    rows = qkv.shape[3]
    length = rows * GROUP
    partners = [member, flip(member, 0), flip(member, 1), 3 - member]
    other_core = {"grp": 1 - core}

    y_place = lax.rem(sequence, y_size)
    ring_place = y_place * GROUP + member
    ring_base = position - ring_place
    x_place = lax.rem(lax.div(sequence, y_size), x_size)
    z_high = lax.div(sequence, y_size * x_size)
    z_place = z_high * dp_size + sample
    z_stride = GROUP * y_size * x_size
    rounds = [
        (
            z_place,
            z_size * dp_size,
            z_slots,
            lambda p: {
                "seq": position + (lax.div(p, dp_size) - z_high) * z_stride,
                "dp": lax.rem(p, dp_size),
            },
        ),
        (
            x_place,
            x_size,
            x_slots,
            lambda p: {"seq": position + (p - x_place) * GROUP * y_size},
        ),
        (ring_place, GROUP * y_size, y_slots, lambda p: {"seq": ring_base + p}),
    ]

    def rows_of(which):
        return pl.ds(pl.multiple_of(which * rows, 16), rows)

    def columns_of(which, head):
        return pl.ds(pl.multiple_of((which * heads + head) * HD, HD), HD)

    def remote(src, dst, send_sem, recv_sem, device):
        return pltpu.make_async_remote_copy(
            src_ref=src,
            dst_ref=dst,
            send_sem=send_sem,
            recv_sem=recv_sem,
            device_id=device,
            device_id_type=MESH,
        )

    def in_pair(head, k):
        theirs = columns_of(partners[k], head)
        mine = rows_of(member)
        ends = (
            (qkv.at[0, :, 0, :, theirs], held.at[head, pl.ds(0, 3), mine, :]),
            (cot.at[0, 0, :, theirs], held.at[head, 3, mine, :]),
        )
        if k == 0:
            return [
                pltpu.make_async_copy(src, dst, in_recv.at[head, k, t])
                for t, (src, dst) in enumerate(ends)
            ]
        return [
            remote(
                src,
                dst,
                in_send.at[head, k, t],
                in_recv.at[head, k, t],
                {"seq": base + partners[k]},
            )
            for t, (src, dst) in enumerate(ends)
        ]

    def in_arrival(head, k):
        theirs = rows_of(partners[k])
        return [
            remote(
                dst,
                dst,
                in_send.at[head, k, t],
                in_recv.at[head, k, t],
                {"seq": base + partners[k]},
            )
            for t, dst in enumerate(
                (held.at[head, pl.ds(0, 3), theirs, :], held.at[head, 3, theirs, :])
            )
        ]

    def out_pair(head, k, t):
        theirs = rows_of(partners[k])
        mine = columns_of(member, head)
        if t == 0:
            src, dst = made.at[head, 0, theirs, :], blended.at[0, 0, :, mine]
        else:
            src, dst = made.at[head, pl.ds(1, 3), theirs, :], grads.at[0, :, 0, :, mine]
        if k == 0:
            return pltpu.make_async_copy(src, dst, out_recv.at[head, k, t])
        return remote(
            src,
            dst,
            out_send.at[head, k, t],
            out_recv.at[head, k, t],
            {"seq": base + partners[k]},
        )

    def out_arrival(head, k, t):
        theirs = columns_of(partners[k], head)
        dst = blended.at[0, 0, :, theirs] if t == 0 else grads.at[0, :, 0, :, theirs]
        return remote(
            dst,
            dst,
            out_send.at[head, k, t],
            out_recv.at[head, k, t],
            {"seq": base + partners[k]},
        )

    def back_copy(head):
        return remote(
            back_out.at[head],
            back_in.at[head],
            back_sems.at[head, 0],
            back_sems.at[head, 1],
            other_core,
        )

    def res_copy(head):
        return remote(
            res_out.at[head],
            res_in.at[head],
            res_sems.at[head, 0],
            res_sems.at[head, 1],
            other_core,
        )

    total_copy = remote(total, total, total_sems.at[0], total_sems.at[1], other_core)

    def round_copies(which):
        place, number, slots, device = rounds[which]
        return [
            remote(
                slots.at[place],
                slots.at[place],
                round_send.at[which, ahead],
                round_recv.at[which, ahead],
                device(lax.rem(place + ahead, number)),
            )
            for ahead in range(1, number)
        ]

    def round_start(which, mine):
        place, _, slots, _ = rounds[which]
        slots[place] = mine
        for copy in round_copies(which):
            copy.start()

    def round_finish(which):
        place, number, slots, device = rounds[which]
        for ahead in range(1, number):
            sender = lax.rem(place + number - ahead, number)
            remote(
                slots.at[sender],
                slots.at[sender],
                round_send.at[which, ahead],
                round_recv.at[which, ahead],
                device(sender),
            ).wait_recv()
        for copy in round_copies(which):
            copy.wait_send()

    def slot_sum(which):
        _, number, slots, _ = rounds[which]
        added = slots[0]
        for slot in range(1, number):
            added = added + slots[slot]
        return added

    small = [
        pltpu.make_async_copy(src, dst, small_sems.at[i])
        for i, (src, dst) in enumerate(
            ((tile_map, order_all), (gate, gains_all), (text_count, counts))
        )
    ]
    for copy in small:
        copy.start()
    for head in range(heads):
        for copy in in_pair(head, 0):
            copy.start()

    barrier = pltpu.get_barrier_semaphore()
    near = [{"seq": base + partners[k]} for k in (1, 2, 3)] + [other_core]
    for peer in near:
        pl.semaphore_signal(barrier, inc=1, device_id=peer, device_id_type=MESH)

    @pl.when(core == 0)
    def _():
        far = []
        for place, number, _, device in rounds[:2]:
            far += [device(lax.rem(place + ahead, number)) for ahead in range(1, number)]
        if y_size == 2:
            far += [{"seq": ring_base + (1 - y_place) * GROUP + k} for k in range(GROUP)]
        for peer in far:
            pl.semaphore_signal(barrier, inc=1, device_id=peer, device_id_type=MESH)
        pl.semaphore_wait(barrier, len(near) + len(far))

    @pl.when(core == 1)
    def _():
        pl.semaphore_wait(barrier, len(near))

    for head in range(heads - 1):
        for k in (2, 3, 1):
            for copy in in_pair(head, k):
                copy.start()

    for copy in small:
        copy.wait()
    partial[...] = jnp.zeros(partial.shape, F32)
    counted = counts[0, sequence]

    @pl.when(core == 1)
    def _():
        order = order_all[0, pl.ds(sequence, 1), :].astype(F32)
        down = lax.broadcasted_iota(jnp.int32, (length, length), 0).astype(F32)
        perm_t[...] = jnp.where(down == order, 1.0, 0.0).astype(BF16)
        order_down = jnp.transpose(jnp.broadcast_to(order, (HD, length)))
        for start in range(0, length, HD):
            width = min(HD, length - start)
            across = lax.broadcasted_iota(jnp.int32, (length, width), 1).astype(F32) + start
            perm[:, start : start + width] = jnp.where(
                order_down[:, :width] == across, 1.0, 0.0
            ).astype(BF16)

    for k in (2, 3, 1):
        for copy in in_pair(0, k):
            copy.wait_send()
    for k in (2, 3, 1):
        for copy in in_pair(heads - 1, k):
            copy.start()

    def arrive(head):
        for k in range(GROUP):
            for copy in in_pair(head, k) if k == 0 else in_arrival(head, k):
                if k == 0:
                    copy.wait()
                else:
                    copy.wait_recv()

        @pl.when(core == 1)
        def _():
            back_out[head] = contract(perm[...], held[head, 3], 1, 0).astype(BF16)
            back_copy(head).start()

    def depart(head):
        for k in (2, 3, 1, 0):
            out_pair(head, k, 1).start()

        @pl.when(core == 1)
        def _():
            res_copy(head).wait_recv()
            placed = contract(perm_t[...], res_in[head], 1, 0)
            made[head, 0] = (made[head, 0].astype(F32) + placed).astype(BF16)

        for k in (2, 3, 1, 0):
            out_pair(head, k, 0).start()

    for head in range(heads - 1):
        arrive(head)

    blocks = [(start, min(BLOCK, length - start)) for start in range(0, length, BLOCK)]

    def one_head(head, carry):
        @pl.when(head == heads - 1)
        def _():
            arrive(head)

        gains = gains_all[pl.ds(member * heads + head, 1), :]
        keys = held[head, 1]
        values = held[head, 2]
        for start, width in blocks:
            span = pl.ds(start, width)
            scores = contract(keys, held[head, 0, span, :], 1, 1)
            text = lax.broadcasted_iota(jnp.int32, (TXT, width), 0) < counted
            scores = jnp.concatenate(
                [jnp.where(text, scores[:TXT], -jnp.inf), scores[TXT:]], axis=0
            )
            top = jnp.max(scores, axis=0, keepdims=True)
            grown = jnp.exp2((scores - top) * EXP2_SCALE)
            probs = grown * (1.0 / jnp.sum(grown, axis=0, keepdims=True))
            probs_low = probs.astype(BF16)
            probs_all[:, start : start + width] = probs
            probs_low_all[:, start : start + width] = probs_low
            made[head, 0, span, :] = jnp.transpose(contract(values, probs_low, 0, 0)).astype(BF16)

        @pl.when(core == 0)
        def _():
            own = made[head, 0].astype(F32)
            res_out[head] = (gains * own).astype(BF16)
            res_copy(head).start()
            back_copy(head).wait_recv()
            back = back_in[head].astype(F32)
            partial[pl.ds(head, 1), :] = jnp.sum(own * back, axis=0, keepdims=True)
            held[head, 3] = (held[head, 3].astype(F32) + gains * back).astype(BF16)

            @pl.when(head == heads - 1)
            def _():
                round_start(0, partial[...])
                round_finish(0)
                round_start(1, slot_sum(0))
                round_finish(1)
                round_start(2, slot_sum(1))

        key_sum = value_sum = None
        for start, width in blocks:
            span = pl.ds(start, width)
            queries = held[head, 0, span, :]
            grad = held[head, 3, span, :]
            probs = probs_all[:, start : start + width]
            grad_probs = contract(values, grad, 1, 1)
            centre = jnp.sum(probs * grad_probs, axis=0, keepdims=True)
            shifted = (probs * (grad_probs - centre)).astype(BF16)
            made[head, 1, span, :] = (
                jnp.transpose(contract(keys, shifted, 0, 0)) * SCALE
            ).astype(BF16)
            key_part = contract(shifted, queries, 1, 0)
            value_part = contract(probs_low_all[:, start : start + width], grad, 1, 0)
            key_sum = key_part if key_sum is None else key_sum + key_part
            value_sum = value_part if value_sum is None else value_sum + value_part
        made[head, 2] = (key_sum * SCALE).astype(BF16)
        made[head, 3] = value_sum.astype(BF16)

        @pl.when(head == heads - 2)
        def _():
            for later in range(1, heads):
                for k in (2, 3, 1):
                    for copy in in_pair(later, k):
                        copy.wait_send()
            for earlier in range(heads - 1):
                depart(earlier)

        @pl.when(head == heads - 1)
        def _():
            depart(head)

        return carry

    lax.fori_loop(0, heads, one_head, 0)

    @pl.when(core == 0)
    def _():
        round_finish(2)
        for which in range(GROUP):
            added = y_slots[which, :heads, :]
            for half in range(1, y_size):
                added = added + y_slots[half * GROUP + which, :heads, :]
            total[which * heads : (which + 1) * heads, :] = added
        total_copy.start()
        total_copy.wait_send()

    @pl.when(core == 1)
    def _():
        total_copy.wait_recv()

    gate_grad[...] = total[...]

    def finish(head, carry):
        for t in (0, 1):
            out_pair(head, 0, t).wait()
            for k in (1, 2, 3):
                out_pair(head, k, t).wait_send()
                out_arrival(head, k, t).wait_recv()

        @pl.when(core == 0)
        def _():
            res_copy(head).wait_send()

        @pl.when(core == 1)
        def _():
            back_copy(head).wait_send()

        return carry

    lax.fori_loop(0, heads, finish, 0)


def per_device(mesh, qkv, cotangent, gate, tile_map, text_count):
    rows, channels = qkv.shape[3:]
    length = rows * GROUP
    heads = channels // HD // GROUP
    groups = mesh.shape["seq"] // GROUP
    dp_size = mesh.shape["dp"]
    y_size = min(2, groups)
    x_size = min(4, groups // y_size)
    z_size = groups // (y_size * x_size)
    places = max(z_size * dp_size, x_size, GROUP * y_size)
    vmem = pl.BlockSpec(memory_space=pltpu.VMEM)
    hbm = pl.BlockSpec(memory_space=pltpu.HBM)
    any_space = pl.BlockSpec(memory_space=pl.ANY)
    dma = pltpu.SemaphoreType.DMA
    blended, grads, gate_grad = pl.pallas_call(
        functools.partial(kernel, heads, (z_size, dp_size, x_size, y_size)),
        out_shape=(
            jax.ShapeDtypeStruct(cotangent.shape, BF16),
            jax.ShapeDtypeStruct(qkv.shape, BF16),
            jax.ShapeDtypeStruct((channels // HD, HD), F32),
        ),
        in_specs=[hbm] * 5,
        out_specs=(any_space, any_space, vmem),
        scratch_shapes=[
            pltpu.VMEM((heads, 4, length, HD), BF16),
            pltpu.VMEM((heads, 4, length, HD), BF16),
            pltpu.VMEM((heads, length, HD), BF16),
            pltpu.VMEM((heads, length, HD), BF16),
            pltpu.VMEM((heads, length, HD), BF16),
            pltpu.VMEM((heads, length, HD), BF16),
            pltpu.VMEM((length, length), BF16),
            pltpu.VMEM((length, length), BF16),
            pltpu.VMEM((length, length), F32),
            pltpu.VMEM((length, length), BF16),
            pltpu.VMEM(tile_map.shape, jnp.int32),
            pltpu.VMEM((channels // HD, HD), F32),
            pltpu.SMEM(text_count.shape, jnp.int32),
            pltpu.VMEM((8, HD), F32),
            pltpu.VMEM((z_size * dp_size, 8, HD), F32),
            pltpu.VMEM((x_size, 8, HD), F32),
            pltpu.VMEM((GROUP * y_size, 8, HD), F32),
            pltpu.VMEM((channels // HD, HD), F32),
            dma((heads, GROUP, 2)),
            dma((heads, GROUP, 2)),
            dma((heads, GROUP, 2)),
            dma((heads, GROUP, 2)),
            dma((heads, 2)),
            dma((heads, 2)),
            dma((3, places)),
            dma((3, places)),
            dma((2,)),
            dma((3,)),
        ],
        compiler_params=pltpu.CompilerParams(
            collective_id=0, has_side_effects=True, vmem_limit_bytes=60 * 1024 * 1024
        ),
    )(qkv, cotangent, gate.reshape(channels // HD, HD), tile_map, text_count)
    return blended, grads, gate_grad.reshape(channels)


def solution(mesh):
    placed = (
        P("grp", None, "dp", "seq", None),
        P("grp", "dp", "seq", None),
        P(),
        P("dp", None, None),
        P("dp", None),
    )
    return jax.shard_map(
        functools.partial(per_device, mesh),
        mesh=mesh,
        in_specs=placed,
        out_specs=(P("grp", "dp", "seq", None), P("grp", None, "dp", "seq", None), P()),
        check_vma=False,
    )
```

```python
import functools
import math

import jax
import jax.numpy as jnp
from jax import lax
from jax.experimental import pallas as pl
from jax.experimental.pallas import tpu as pltpu
from jax.sharding import PartitionSpec as P

HD = 128
GROUP = 4
TXT = 128
BLOCK = 704
SCALE = 1.0 / math.sqrt(HD)
EXP2_SCALE = SCALE * math.log2(math.e)
MESH = pl.DeviceIdType.MESH
BF16 = jnp.bfloat16
F32 = jnp.float32


def flip(index, bit):
    unit = 1 << bit
    return index + unit - 2 * unit * lax.rem(lax.div(index, unit), 2)


def contract(left, right, left_dim, right_dim):
    return lax.dot_general(
        left, right, (((left_dim,), (right_dim,)), ((), ())), preferred_element_type=F32
    )


def kernel(
    heads,
    sizes,
    qkv,
    cot,
    gate,
    tile_map,
    text_count,
    blended,
    grads,
    gate_grad,
    held,
    made,
    back_out,
    back_in,
    res_out,
    res_in,
    perm,
    perm_t,
    probs_all,
    probs_low_all,
    order_all,
    gains_all,
    counts,
    partial,
    z_slots,
    x_slots,
    y_slots,
    total,
    in_send,
    in_recv,
    out_send,
    out_recv,
    back_sems,
    res_sems,
    round_send,
    round_recv,
    total_sems,
    small_sems,
):
    z_size, dp_size, x_size, y_size = sizes
    core = lax.axis_index("grp")
    position = lax.axis_index("seq")
    sample = lax.axis_index("dp")
    member = lax.rem(position, GROUP)
    sequence = lax.div(position, GROUP)
    base = position - member
    rows = qkv.shape[3]
    length = rows * GROUP
    partners = [member, flip(member, 0), flip(member, 1), 3 - member]
    other_core = {"grp": 1 - core}

    y_place = lax.rem(sequence, y_size)
    ring_place = y_place * GROUP + member
    ring_base = position - ring_place
    x_place = lax.rem(lax.div(sequence, y_size), x_size)
    z_high = lax.div(sequence, y_size * x_size)
    z_place = z_high * dp_size + sample
    z_stride = GROUP * y_size * x_size
    rounds = [
        (
            z_place,
            z_size * dp_size,
            z_slots,
            lambda p: {
                "seq": position + (lax.div(p, dp_size) - z_high) * z_stride,
                "dp": lax.rem(p, dp_size),
            },
        ),
        (
            x_place,
            x_size,
            x_slots,
            lambda p: {"seq": position + (p - x_place) * GROUP * y_size},
        ),
        (ring_place, GROUP * y_size, y_slots, lambda p: {"seq": ring_base + p}),
    ]

    def rows_of(which):
        return pl.ds(pl.multiple_of(which * rows, 16), rows)

    def columns_of(which, head):
        return pl.ds(pl.multiple_of((which * heads + head) * HD, HD), HD)

    def remote(src, dst, send_sem, recv_sem, device):
        return pltpu.make_async_remote_copy(
            src_ref=src,
            dst_ref=dst,
            send_sem=send_sem,
            recv_sem=recv_sem,
            device_id=device,
            device_id_type=MESH,
        )

    def in_pair(head, k):
        theirs = columns_of(partners[k], head)
        mine = rows_of(member)
        ends = (
            (qkv.at[0, :, 0, :, theirs], held.at[head, pl.ds(0, 3), mine, :]),
            (cot.at[0, 0, :, theirs], held.at[head, 3, mine, :]),
        )
        if k == 0:
            return [
                pltpu.make_async_copy(src, dst, in_recv.at[head, k, t])
                for t, (src, dst) in enumerate(ends)
            ]
        return [
            remote(
                src,
                dst,
                in_send.at[head, k, t],
                in_recv.at[head, k, t],
                {"seq": base + partners[k]},
            )
            for t, (src, dst) in enumerate(ends)
        ]

    def in_arrival(head, k):
        theirs = rows_of(partners[k])
        return [
            remote(
                dst,
                dst,
                in_send.at[head, k, t],
                in_recv.at[head, k, t],
                {"seq": base + partners[k]},
            )
            for t, dst in enumerate(
                (held.at[head, pl.ds(0, 3), theirs, :], held.at[head, 3, theirs, :])
            )
        ]

    def out_pair(head, k, t):
        theirs = rows_of(partners[k])
        mine = columns_of(member, head)
        if t == 0:
            src, dst = made.at[head, 0, theirs, :], blended.at[0, 0, :, mine]
        else:
            src, dst = made.at[head, pl.ds(1, 3), theirs, :], grads.at[0, :, 0, :, mine]
        if k == 0:
            return pltpu.make_async_copy(src, dst, out_recv.at[head, k, t])
        return remote(
            src,
            dst,
            out_send.at[head, k, t],
            out_recv.at[head, k, t],
            {"seq": base + partners[k]},
        )

    def out_arrival(head, k, t):
        theirs = columns_of(partners[k], head)
        dst = blended.at[0, 0, :, theirs] if t == 0 else grads.at[0, :, 0, :, theirs]
        return remote(
            dst,
            dst,
            out_send.at[head, k, t],
            out_recv.at[head, k, t],
            {"seq": base + partners[k]},
        )

    def back_copy(head):
        return remote(
            back_out.at[head],
            back_in.at[head],
            back_sems.at[head, 0],
            back_sems.at[head, 1],
            other_core,
        )

    def res_copy(head):
        return remote(
            res_out.at[head],
            res_in.at[head],
            res_sems.at[head, 0],
            res_sems.at[head, 1],
            other_core,
        )

    total_copy = remote(total, total, total_sems.at[0], total_sems.at[1], other_core)

    def round_copies(which):
        place, number, slots, device = rounds[which]
        return [
            remote(
                slots.at[place],
                slots.at[place],
                round_send.at[which, ahead],
                round_recv.at[which, ahead],
                device(lax.rem(place + ahead, number)),
            )
            for ahead in range(1, number)
        ]

    def round_start(which, mine):
        place, _, slots, _ = rounds[which]
        slots[place] = mine
        for copy in round_copies(which):
            copy.start()

    def round_finish(which):
        place, number, slots, device = rounds[which]
        for ahead in range(1, number):
            sender = lax.rem(place + number - ahead, number)
            remote(
                slots.at[sender],
                slots.at[sender],
                round_send.at[which, ahead],
                round_recv.at[which, ahead],
                device(sender),
            ).wait_recv()
        for copy in round_copies(which):
            copy.wait_send()

    def slot_sum(which):
        _, number, slots, _ = rounds[which]
        added = slots[0]
        for slot in range(1, number):
            added = added + slots[slot]
        return added

    small = [
        pltpu.make_async_copy(src, dst, small_sems.at[i])
        for i, (src, dst) in enumerate(
            ((tile_map, order_all), (gate, gains_all), (text_count, counts))
        )
    ]
    for copy in small:
        copy.start()
    for head in range(heads):
        for copy in in_pair(head, 0):
            copy.start()

    barrier = pltpu.get_barrier_semaphore()
    near = [{"seq": base + partners[k]} for k in (1, 2, 3)] + [other_core]
    for peer in near:
        pl.semaphore_signal(barrier, inc=1, device_id=peer, device_id_type=MESH)

    @pl.when(core == 0)
    def _():
        far = []
        for place, number, _, device in rounds[:2]:
            far += [device(lax.rem(place + ahead, number)) for ahead in range(1, number)]
        if y_size == 2:
            far += [{"seq": ring_base + (1 - y_place) * GROUP + k} for k in range(GROUP)]
        for peer in far:
            pl.semaphore_signal(barrier, inc=1, device_id=peer, device_id_type=MESH)
        pl.semaphore_wait(barrier, len(near) + len(far))

    @pl.when(core == 1)
    def _():
        pl.semaphore_wait(barrier, len(near))

    for head in range(heads - 1):
        for k in (2, 3, 1):
            for copy in in_pair(head, k):
                copy.start()

    for copy in small:
        copy.wait()
    partial[...] = jnp.zeros(partial.shape, F32)
    counted = counts[0, sequence]

    @pl.when(core == 1)
    def _():
        order = order_all[0, pl.ds(sequence, 1), :].astype(F32)
        down = lax.broadcasted_iota(jnp.int32, (length, length), 0).astype(F32)
        perm_t[...] = jnp.where(down == order, 1.0, 0.0).astype(BF16)
        order_down = jnp.transpose(jnp.broadcast_to(order, (HD, length)))
        for start in range(0, length, HD):
            width = min(HD, length - start)
            across = lax.broadcasted_iota(jnp.int32, (length, width), 1).astype(F32) + start
            perm[:, start : start + width] = jnp.where(
                order_down[:, :width] == across, 1.0, 0.0
            ).astype(BF16)

    for k in (2, 3, 1):
        for copy in in_pair(0, k):
            copy.wait_send()
    for k in (2, 3, 1):
        for copy in in_pair(heads - 1, k):
            copy.start()

    def arrive(head):
        for k in range(GROUP):
            for copy in in_pair(head, k) if k == 0 else in_arrival(head, k):
                if k == 0:
                    copy.wait()
                else:
                    copy.wait_recv()

        @pl.when(core == 1)
        def _():
            back_out[head] = contract(perm[...], held[head, 3], 1, 0).astype(BF16)
            back_copy(head).start()

    def depart(head):
        for k in (2, 3, 1, 0):
            out_pair(head, k, 1).start()

        @pl.when(core == 1)
        def _():
            res_copy(head).wait_recv()
            placed = contract(perm_t[...], res_in[head], 1, 0)
            made[head, 0] = (made[head, 0].astype(F32) + placed).astype(BF16)

        for k in (2, 3, 1, 0):
            out_pair(head, k, 0).start()

    for head in range(heads - 1):
        arrive(head)

    blocks = [(start, min(BLOCK, length - start)) for start in range(0, length, BLOCK)]

    def one_head(head, carry):
        @pl.when(head == heads - 1)
        def _():
            arrive(head)

        gains = gains_all[pl.ds(member * heads + head, 1), :]
        keys = held[head, 1]
        values = held[head, 2]
        for start, width in blocks:
            span = pl.ds(start, width)
            scores = contract(keys, held[head, 0, span, :], 1, 1)
            text = lax.broadcasted_iota(jnp.int32, (TXT, width), 0) < counted
            scores = jnp.concatenate(
                [jnp.where(text, scores[:TXT], -jnp.inf), scores[TXT:]], axis=0
            )
            top = jnp.max(scores, axis=0, keepdims=True)
            grown = jnp.exp2((scores - top) * EXP2_SCALE)
            probs = grown * (1.0 / jnp.sum(grown, axis=0, keepdims=True))
            probs_low = probs.astype(BF16)
            probs_all[:, start : start + width] = probs
            probs_low_all[:, start : start + width] = probs_low
            made[head, 0, span, :] = jnp.transpose(contract(values, probs_low, 0, 0)).astype(BF16)

        @pl.when(core == 0)
        def _():
            own = made[head, 0].astype(F32)
            res_out[head] = (gains * own).astype(BF16)
            res_copy(head).start()
            back_copy(head).wait_recv()
            back = back_in[head].astype(F32)
            partial[pl.ds(head, 1), :] = jnp.sum(own * back, axis=0, keepdims=True)
            held[head, 3] = (held[head, 3].astype(F32) + gains * back).astype(BF16)

            @pl.when(head == heads - 1)
            def _():
                round_start(0, partial[...])
                round_finish(0)
                round_start(1, slot_sum(0))
                round_finish(1)
                round_start(2, slot_sum(1))

        key_sum = value_sum = None
        for start, width in blocks:
            span = pl.ds(start, width)
            queries = held[head, 0, span, :]
            grad = held[head, 3, span, :]
            probs = probs_all[:, start : start + width]
            grad_probs = contract(values, grad, 1, 1)
            centre = jnp.sum(probs * grad_probs, axis=0, keepdims=True)
            shifted = (probs * (grad_probs - centre)).astype(BF16)
            made[head, 1, span, :] = (
                jnp.transpose(contract(keys, shifted, 0, 0)) * SCALE
            ).astype(BF16)
            key_part = contract(shifted, queries, 1, 0)
            value_part = contract(probs_low_all[:, start : start + width], grad, 1, 0)
            key_sum = key_part if key_sum is None else key_sum + key_part
            value_sum = value_part if value_sum is None else value_sum + value_part
        made[head, 2] = (key_sum * SCALE).astype(BF16)
        made[head, 3] = value_sum.astype(BF16)

        @pl.when(head == heads - 2)
        def _():
            for later in range(1, heads):
                for k in (2, 3, 1):
                    for copy in in_pair(later, k):
                        copy.wait_send()
            for earlier in range(heads - 1):
                depart(earlier)

        @pl.when(head == heads - 1)
        def _():
            depart(head)

        return carry

    lax.fori_loop(0, heads, one_head, 0)

    @pl.when(core == 0)
    def _():
        round_finish(2)
        for which in range(GROUP):
            added = y_slots[which, :heads, :]
            for half in range(1, y_size):
                added = added + y_slots[half * GROUP + which, :heads, :]
            total[which * heads : (which + 1) * heads, :] = added
        total_copy.start()
        total_copy.wait_send()

    @pl.when(core == 1)
    def _():
        total_copy.wait_recv()

    gate_grad[...] = total[...]

    def finish(head, carry):
        for t in (0, 1):
            out_pair(head, 0, t).wait()
            for k in (1, 2, 3):
                out_pair(head, k, t).wait_send()
                out_arrival(head, k, t).wait_recv()

        @pl.when(core == 0)
        def _():
            res_copy(head).wait_send()

        @pl.when(core == 1)
        def _():
            back_copy(head).wait_send()

        return carry

    lax.fori_loop(0, heads, finish, 0)


def store(*refs):
    sems = refs[-1]
    number = len(refs) // 2
    copies = [
        pltpu.make_async_copy(refs[i], refs[number + i], sems.at[i]) for i in range(number)
    ]
    for copy in copies:
        copy.start()
    for copy in copies:
        copy.wait()


def per_device(mesh, qkv, cotangent, gate, tile_map, text_count):
    rows, channels = qkv.shape[3:]
    length = rows * GROUP
    heads = channels // HD // GROUP
    groups = mesh.shape["seq"] // GROUP
    dp_size = mesh.shape["dp"]
    y_size = min(2, groups)
    x_size = min(4, groups // y_size)
    z_size = groups // (y_size * x_size)
    places = max(z_size * dp_size, x_size, GROUP * y_size)
    vmem = pl.BlockSpec(memory_space=pltpu.VMEM)
    hbm = pl.BlockSpec(memory_space=pltpu.HBM)
    any_space = pl.BlockSpec(memory_space=pl.ANY)
    dma = pltpu.SemaphoreType.DMA
    blended, grads, gate_grad = pl.pallas_call(
        functools.partial(kernel, heads, (z_size, dp_size, x_size, y_size)),
        out_shape=(
            pltpu.VMEM(cotangent.shape, BF16),
            pltpu.VMEM(qkv.shape, BF16),
            pltpu.VMEM((channels // HD, HD), F32),
        ),
        in_specs=[hbm] * 5,
        out_specs=(any_space, any_space, vmem),
        scratch_shapes=[
            pltpu.VMEM((heads, 4, length, HD), BF16),
            pltpu.VMEM((heads, 4, length, HD), BF16),
            pltpu.VMEM((heads, length, HD), BF16),
            pltpu.VMEM((heads, length, HD), BF16),
            pltpu.VMEM((heads, length, HD), BF16),
            pltpu.VMEM((heads, length, HD), BF16),
            pltpu.VMEM((length, length), BF16),
            pltpu.VMEM((length, length), BF16),
            pltpu.VMEM((length, length), F32),
            pltpu.VMEM((length, length), BF16),
            pltpu.VMEM(tile_map.shape, jnp.int32),
            pltpu.VMEM((channels // HD, HD), F32),
            pltpu.SMEM(text_count.shape, jnp.int32),
            pltpu.VMEM((8, HD), F32),
            pltpu.VMEM((z_size * dp_size, 8, HD), F32),
            pltpu.VMEM((x_size, 8, HD), F32),
            pltpu.VMEM((GROUP * y_size, 8, HD), F32),
            pltpu.VMEM((channels // HD, HD), F32),
            dma((heads, GROUP, 2)),
            dma((heads, GROUP, 2)),
            dma((heads, GROUP, 2)),
            dma((heads, GROUP, 2)),
            dma((heads, 2)),
            dma((heads, 2)),
            dma((3, places)),
            dma((3, places)),
            dma((2,)),
            dma((3,)),
        ],
        compiler_params=pltpu.CompilerParams(
            collective_id=0, has_side_effects=True, vmem_limit_bytes=44 * 1024 * 1024
        ),
    )(
        *(
            pltpu.with_memory_space_constraint(operand, pltpu.HBM)
            for operand in (qkv, cotangent, gate.reshape(channels // HD, HD), tile_map, text_count)
        )
    )
    results = (blended, grads, gate_grad.reshape(channels))
    return pl.pallas_call(
        store,
        out_shape=tuple(pltpu.HBM(result.shape, result.dtype) for result in results),
        in_specs=[any_space] * 3,
        out_specs=(any_space,) * 3,
        scratch_shapes=[dma((3,))],
    )(*(pltpu.with_memory_space_constraint(result, pltpu.VMEM) for result in results))


def solution(mesh):
    placed = (
        P("grp", None, "dp", "seq", None),
        P("grp", "dp", "seq", None),
        P(),
        P("dp", None, None),
        P("dp", None),
    )
    return jax.shard_map(
        functools.partial(per_device, mesh),
        mesh=mesh,
        in_specs=placed,
        out_specs=(P("grp", "dp", "seq", None), P("grp", None, "dp", "seq", None), P()),
        check_vma=False,
    )
```

```python
import functools
import math

import jax
import jax.numpy as jnp
from jax import lax
from jax.experimental import pallas as pl
from jax.experimental.pallas import tpu as pltpu
from jax.sharding import PartitionSpec as P

HD = 128
GROUP = 4
TXT = 128
BLOCK = 704
SCALE = 1.0 / math.sqrt(HD)
EXP2_SCALE = SCALE * math.log2(math.e)
MESH = pl.DeviceIdType.MESH
BF16 = jnp.bfloat16
F32 = jnp.float32


def flip(index, bit):
    unit = 1 << bit
    return index + unit - 2 * unit * lax.rem(lax.div(index, unit), 2)


def contract(left, right, left_dim, right_dim):
    return lax.dot_general(
        left, right, (((left_dim,), (right_dim,)), ((), ())), preferred_element_type=F32
    )


def kernel(
    heads,
    sizes,
    qkv,
    cot,
    gate,
    tile_map,
    text_count,
    blended,
    grads,
    gate_grad,
    held,
    made,
    back_out,
    back_in,
    res_out,
    res_in,
    perm,
    perm_t,
    probs_all,
    probs_low_all,
    order_all,
    gains_all,
    counts,
    partial,
    z_slots,
    x_slots,
    y_slots,
    total,
    in_send,
    in_recv,
    out_send,
    out_recv,
    back_sems,
    res_sems,
    round_send,
    round_recv,
    total_sems,
    small_sems,
):
    z_size, dp_size, x_size, y_size = sizes
    core = lax.axis_index("grp")
    position = lax.axis_index("seq")
    sample = lax.axis_index("dp")
    member = lax.rem(position, GROUP)
    sequence = lax.div(position, GROUP)
    base = position - member
    rows = qkv.shape[3]
    length = rows * GROUP
    partners = [member, flip(member, 0), flip(member, 1), 3 - member]
    other_core = {"grp": 1 - core}

    y_place = lax.rem(sequence, y_size)
    ring_place = y_place * GROUP + member
    ring_base = position - ring_place
    x_place = lax.rem(lax.div(sequence, y_size), x_size)
    z_high = lax.div(sequence, y_size * x_size)
    z_place = z_high * dp_size + sample
    z_stride = GROUP * y_size * x_size
    rounds = [
        (
            z_place,
            z_size * dp_size,
            z_slots,
            lambda p: {
                "seq": position + (lax.div(p, dp_size) - z_high) * z_stride,
                "dp": lax.rem(p, dp_size),
            },
        ),
        (
            x_place,
            x_size,
            x_slots,
            lambda p: {"seq": position + (p - x_place) * GROUP * y_size},
        ),
        (ring_place, GROUP * y_size, y_slots, lambda p: {"seq": ring_base + p}),
    ]

    def rows_of(which):
        return pl.ds(pl.multiple_of(which * rows, 16), rows)

    def columns_of(which, head):
        return pl.ds(pl.multiple_of((which * heads + head) * HD, HD), HD)

    def remote(src, dst, send_sem, recv_sem, device):
        return pltpu.make_async_remote_copy(
            src_ref=src,
            dst_ref=dst,
            send_sem=send_sem,
            recv_sem=recv_sem,
            device_id=device,
            device_id_type=MESH,
        )

    def in_pair(head, k):
        theirs = columns_of(partners[k], head)
        mine = rows_of(member)
        ends = (
            (qkv.at[0, :, 0, :, theirs], held.at[head, pl.ds(0, 3), mine, :]),
            (cot.at[0, 0, :, theirs], held.at[head, 3, mine, :]),
        )
        if k == 0:
            return [
                pltpu.make_async_copy(src, dst, in_recv.at[head, k, t])
                for t, (src, dst) in enumerate(ends)
            ]
        return [
            remote(
                src,
                dst,
                in_send.at[head, k, t],
                in_recv.at[head, k, t],
                {"seq": base + partners[k]},
            )
            for t, (src, dst) in enumerate(ends)
        ]

    def in_arrival(head, k):
        theirs = rows_of(partners[k])
        return [
            remote(
                dst,
                dst,
                in_send.at[head, k, t],
                in_recv.at[head, k, t],
                {"seq": base + partners[k]},
            )
            for t, dst in enumerate(
                (held.at[head, pl.ds(0, 3), theirs, :], held.at[head, 3, theirs, :])
            )
        ]

    def out_pair(head, k, t):
        theirs = rows_of(partners[k])
        mine = columns_of(member, head)
        if t == 0:
            src, dst = made.at[head, 0, theirs, :], blended.at[0, 0, :, mine]
        else:
            src, dst = made.at[head, pl.ds(1, 3), theirs, :], grads.at[0, :, 0, :, mine]
        if k == 0:
            return pltpu.make_async_copy(src, dst, out_recv.at[head, k, t])
        return remote(
            src,
            dst,
            out_send.at[head, k, t],
            out_recv.at[head, k, t],
            {"seq": base + partners[k]},
        )

    def out_arrival(head, k, t):
        theirs = columns_of(partners[k], head)
        dst = blended.at[0, 0, :, theirs] if t == 0 else grads.at[0, :, 0, :, theirs]
        return remote(
            dst,
            dst,
            out_send.at[head, k, t],
            out_recv.at[head, k, t],
            {"seq": base + partners[k]},
        )

    def back_copy(head):
        return remote(
            back_out.at[head],
            back_in.at[head],
            back_sems.at[head, 0],
            back_sems.at[head, 1],
            other_core,
        )

    def res_copy(head):
        return remote(
            res_out.at[head],
            res_in.at[head],
            res_sems.at[head, 0],
            res_sems.at[head, 1],
            other_core,
        )

    total_copy = remote(total, total, total_sems.at[0], total_sems.at[1], other_core)

    def round_copies(which):
        place, number, slots, device = rounds[which]
        return [
            remote(
                slots.at[place],
                slots.at[place],
                round_send.at[which, ahead],
                round_recv.at[which, ahead],
                device(lax.rem(place + ahead, number)),
            )
            for ahead in range(1, number)
        ]

    def round_start(which, mine):
        place, _, slots, _ = rounds[which]
        slots[place] = mine
        for copy in round_copies(which):
            copy.start()

    def round_finish(which):
        place, number, slots, device = rounds[which]
        for ahead in range(1, number):
            sender = lax.rem(place + number - ahead, number)
            remote(
                slots.at[sender],
                slots.at[sender],
                round_send.at[which, ahead],
                round_recv.at[which, ahead],
                device(sender),
            ).wait_recv()
        for copy in round_copies(which):
            copy.wait_send()

    def slot_sum(which):
        _, number, slots, _ = rounds[which]
        added = slots[0]
        for slot in range(1, number):
            added = added + slots[slot]
        return added

    small = [
        pltpu.make_async_copy(src, dst, small_sems.at[i])
        for i, (src, dst) in enumerate(
            ((tile_map, order_all), (gate, gains_all), (text_count, counts))
        )
    ]
    for copy in small:
        copy.start()
    for head in range(heads):
        for copy in in_pair(head, 0):
            copy.start()

    barrier = pltpu.get_barrier_semaphore()
    near = [{"seq": base + partners[k]} for k in (1, 2, 3)] + [other_core]
    for peer in near:
        pl.semaphore_signal(barrier, inc=1, device_id=peer, device_id_type=MESH)

    @pl.when(core == 0)
    def _():
        far = []
        for place, number, _, device in rounds[:2]:
            far += [device(lax.rem(place + ahead, number)) for ahead in range(1, number)]
        if y_size == 2:
            far += [{"seq": ring_base + (1 - y_place) * GROUP + k} for k in range(GROUP)]
        for peer in far:
            pl.semaphore_signal(barrier, inc=1, device_id=peer, device_id_type=MESH)
        pl.semaphore_wait(barrier, len(near) + len(far))

    @pl.when(core == 1)
    def _():
        pl.semaphore_wait(barrier, len(near))

    for head in range(heads - 1):
        for k in (2, 3, 1):
            for copy in in_pair(head, k):
                copy.start()

    for copy in small:
        copy.wait()
    partial[...] = jnp.zeros(partial.shape, F32)
    counted = counts[0, sequence]

    @pl.when(core == 1)
    def _():
        order = order_all[0, pl.ds(sequence, 1), :].astype(F32)
        down = lax.broadcasted_iota(jnp.int32, (length, length), 0).astype(F32)
        perm_t[...] = jnp.where(down == order, 1.0, 0.0).astype(BF16)
        order_down = jnp.transpose(jnp.broadcast_to(order, (HD, length)))
        for start in range(0, length, HD):
            width = min(HD, length - start)
            across = lax.broadcasted_iota(jnp.int32, (length, width), 1).astype(F32) + start
            perm[:, start : start + width] = jnp.where(
                order_down[:, :width] == across, 1.0, 0.0
            ).astype(BF16)

    for k in (2, 3, 1):
        for copy in in_pair(0, k):
            copy.wait_send()
    for k in (2, 3, 1):
        for copy in in_pair(heads - 1, k):
            copy.start()

    def arrive(head):
        for k in range(GROUP):
            for copy in in_pair(head, k) if k == 0 else in_arrival(head, k):
                if k == 0:
                    copy.wait()
                else:
                    copy.wait_recv()

        @pl.when(core == 1)
        def _():
            back_out[head] = contract(perm[...], held[head, 3], 1, 0).astype(BF16)
            back_copy(head).start()

    def depart(head):
        for k in (2, 3, 1, 0):
            out_pair(head, k, 1).start()

        @pl.when(core == 1)
        def _():
            res_copy(head).wait_recv()
            placed = contract(perm_t[...], res_in[head], 1, 0)
            made[head, 0] = (made[head, 0].astype(F32) + placed).astype(BF16)

        for k in (2, 3, 1, 0):
            out_pair(head, k, 0).start()

    for head in range(heads - 1):
        arrive(head)

    blocks = [(start, min(BLOCK, length - start)) for start in range(0, length, BLOCK)]

    def one_head(head, carry):
        @pl.when(head == heads - 1)
        def _():
            arrive(head)

        gains = gains_all[pl.ds(member * heads + head, 1), :]
        keys = held[head, 1]
        values = held[head, 2]
        for start, width in blocks:
            span = pl.ds(start, width)
            scores = contract(keys, held[head, 0, span, :], 1, 1)
            text = lax.broadcasted_iota(jnp.int32, (TXT, width), 0) < counted
            scores = jnp.concatenate(
                [jnp.where(text, scores[:TXT], -jnp.inf), scores[TXT:]], axis=0
            )
            top = jnp.max(scores, axis=0, keepdims=True)
            grown = jnp.exp2((scores - top) * EXP2_SCALE)
            probs = grown * (1.0 / jnp.sum(grown, axis=0, keepdims=True))
            probs_low = probs.astype(BF16)
            probs_all[:, start : start + width] = probs
            probs_low_all[:, start : start + width] = probs_low
            made[head, 0, span, :] = jnp.transpose(contract(values, probs_low, 0, 0)).astype(BF16)

        @pl.when(core == 0)
        def _():
            own = made[head, 0].astype(F32)
            res_out[head] = (gains * own).astype(BF16)
            res_copy(head).start()
            back_copy(head).wait_recv()
            back = back_in[head].astype(F32)
            partial[pl.ds(head, 1), :] = jnp.sum(own * back, axis=0, keepdims=True)
            held[head, 3] = (held[head, 3].astype(F32) + gains * back).astype(BF16)

            @pl.when(head == heads - 1)
            def _():
                round_start(0, partial[...])

        key_sum = value_sum = None
        for start, width in blocks:
            span = pl.ds(start, width)
            queries = held[head, 0, span, :]
            grad = held[head, 3, span, :]
            probs = probs_all[:, start : start + width]
            grad_probs = contract(values, grad, 1, 1)
            centre = jnp.sum(probs * grad_probs, axis=0, keepdims=True)
            shifted = (probs * (grad_probs - centre)).astype(BF16)
            made[head, 1, span, :] = (
                jnp.transpose(contract(keys, shifted, 0, 0)) * SCALE
            ).astype(BF16)
            key_part = contract(shifted, queries, 1, 0)
            value_part = contract(probs_low_all[:, start : start + width], grad, 1, 0)
            key_sum = key_part if key_sum is None else key_sum + key_part
            value_sum = value_part if value_sum is None else value_sum + value_part
        made[head, 2] = (key_sum * SCALE).astype(BF16)
        made[head, 3] = value_sum.astype(BF16)

        @pl.when((core == 0) & (head == heads - 1))
        def _():
            round_finish(0)
            round_start(1, slot_sum(0))
            round_finish(1)
            round_start(2, slot_sum(1))

        depart(head)

        return carry

    lax.fori_loop(0, heads, one_head, 0)

    @pl.when(core == 0)
    def _():
        round_finish(2)
        for which in range(GROUP):
            added = y_slots[which, :heads, :]
            for half in range(1, y_size):
                added = added + y_slots[half * GROUP + which, :heads, :]
            total[which * heads : (which + 1) * heads, :] = added
        total_copy.start()
        total_copy.wait_send()

    @pl.when(core == 1)
    def _():
        total_copy.wait_recv()

    gate_grad[...] = total[...]

    def finish(head, carry):
        @pl.when(head > 0)
        def _():
            for k in (1, 2, 3):
                for copy in in_pair(head, k):
                    copy.wait_send()

        for t in (0, 1):
            out_pair(head, 0, t).wait()
            for k in (1, 2, 3):
                out_pair(head, k, t).wait_send()
                out_arrival(head, k, t).wait_recv()

        @pl.when(core == 0)
        def _():
            res_copy(head).wait_send()

        @pl.when(core == 1)
        def _():
            back_copy(head).wait_send()

        return carry

    lax.fori_loop(0, heads, finish, 0)


def store(*refs):
    sems = refs[-1]
    number = len(refs) // 2
    copies = [
        pltpu.make_async_copy(refs[i], refs[number + i], sems.at[i]) for i in range(number)
    ]
    for copy in copies:
        copy.start()
    for copy in copies:
        copy.wait()


def per_device(mesh, qkv, cotangent, gate, tile_map, text_count):
    rows, channels = qkv.shape[3:]
    length = rows * GROUP
    heads = channels // HD // GROUP
    groups = mesh.shape["seq"] // GROUP
    dp_size = mesh.shape["dp"]
    y_size = min(2, groups)
    x_size = min(4, groups // y_size)
    z_size = groups // (y_size * x_size)
    places = max(z_size * dp_size, x_size, GROUP * y_size)
    vmem = pl.BlockSpec(memory_space=pltpu.VMEM)
    hbm = pl.BlockSpec(memory_space=pltpu.HBM)
    any_space = pl.BlockSpec(memory_space=pl.ANY)
    dma = pltpu.SemaphoreType.DMA
    blended, grads, gate_grad = pl.pallas_call(
        functools.partial(kernel, heads, (z_size, dp_size, x_size, y_size)),
        out_shape=(
            pltpu.VMEM(cotangent.shape, BF16),
            pltpu.VMEM(qkv.shape, BF16),
            pltpu.VMEM((channels // HD, HD), F32),
        ),
        in_specs=[hbm] * 5,
        out_specs=(any_space, any_space, vmem),
        scratch_shapes=[
            pltpu.VMEM((heads, 4, length, HD), BF16),
            pltpu.VMEM((heads, 4, length, HD), BF16),
            pltpu.VMEM((heads, length, HD), BF16),
            pltpu.VMEM((heads, length, HD), BF16),
            pltpu.VMEM((heads, length, HD), BF16),
            pltpu.VMEM((heads, length, HD), BF16),
            pltpu.VMEM((length, length), BF16),
            pltpu.VMEM((length, length), BF16),
            pltpu.VMEM((length, length), F32),
            pltpu.VMEM((length, length), BF16),
            pltpu.VMEM(tile_map.shape, jnp.int32),
            pltpu.VMEM((channels // HD, HD), F32),
            pltpu.SMEM(text_count.shape, jnp.int32),
            pltpu.VMEM((8, HD), F32),
            pltpu.VMEM((z_size * dp_size, 8, HD), F32),
            pltpu.VMEM((x_size, 8, HD), F32),
            pltpu.VMEM((GROUP * y_size, 8, HD), F32),
            pltpu.VMEM((channels // HD, HD), F32),
            dma((heads, GROUP, 2)),
            dma((heads, GROUP, 2)),
            dma((heads, GROUP, 2)),
            dma((heads, GROUP, 2)),
            dma((heads, 2)),
            dma((heads, 2)),
            dma((3, places)),
            dma((3, places)),
            dma((2,)),
            dma((3,)),
        ],
        compiler_params=pltpu.CompilerParams(
            collective_id=0, has_side_effects=True, vmem_limit_bytes=44 * 1024 * 1024
        ),
    )(
        *(
            pltpu.with_memory_space_constraint(operand, pltpu.HBM)
            for operand in (qkv, cotangent, gate.reshape(channels // HD, HD), tile_map, text_count)
        )
    )
    results = (blended, grads, gate_grad.reshape(channels))
    return pl.pallas_call(
        store,
        out_shape=tuple(pltpu.HBM(result.shape, result.dtype) for result in results),
        in_specs=[any_space] * 3,
        out_specs=(any_space,) * 3,
        scratch_shapes=[dma((3,))],
    )(*(pltpu.with_memory_space_constraint(result, pltpu.VMEM) for result in results))


def solution(mesh):
    placed = (
        P("grp", None, "dp", "seq", None),
        P("grp", "dp", "seq", None),
        P(),
        P("dp", None, None),
        P("dp", None),
    )
    return jax.shard_map(
        functools.partial(per_device, mesh),
        mesh=mesh,
        in_specs=placed,
        out_specs=(P("grp", "dp", "seq", None), P("grp", None, "dp", "seq", None), P()),
        check_vma=False,
    )
```

```python
import functools
import math

import jax
import jax.numpy as jnp
from jax import lax
from jax.experimental import pallas as pl
from jax.experimental.pallas import tpu as pltpu
from jax.sharding import PartitionSpec as P

HD = 128
GROUP = 4
TXT = 128
BLOCK = 704
SCALE = 1.0 / math.sqrt(HD)
EXP2_SCALE = SCALE * math.log2(math.e)
MESH = pl.DeviceIdType.MESH
BF16 = jnp.bfloat16
F32 = jnp.float32


def flip(index, bit):
    unit = 1 << bit
    return index + unit - 2 * unit * lax.rem(lax.div(index, unit), 2)


def contract(left, right, left_dim, right_dim):
    return lax.dot_general(
        left, right, (((left_dim,), (right_dim,)), ((), ())), preferred_element_type=F32
    )


def kernel(
    heads,
    sizes,
    qkv,
    cot,
    gate,
    tile_map,
    text_count,
    blended,
    grads,
    gate_grad,
    held,
    made,
    back_out,
    back_in,
    res_out,
    res_in,
    perm,
    perm_t,
    probs_all,
    probs_low_all,
    order_all,
    gains_all,
    counts,
    partial,
    z_slots,
    x_slots,
    y_slots,
    total,
    in_send,
    in_recv,
    out_send,
    out_recv,
    back_sems,
    res_sems,
    round_send,
    round_recv,
    total_sems,
    small_sems,
    entered,
    known,
):
    z_size, dp_size, x_size, y_size = sizes
    core = lax.axis_index("grp")
    position = lax.axis_index("seq")
    sample = lax.axis_index("dp")
    member = lax.rem(position, GROUP)
    sequence = lax.div(position, GROUP)
    base = position - member
    rows = qkv.shape[3]
    length = rows * GROUP
    partners = [member, flip(member, 0), flip(member, 1), 3 - member]
    other_core = {"grp": 1 - core}

    y_place = lax.rem(sequence, y_size)
    ring_place = y_place * GROUP + member
    ring_base = position - ring_place
    x_place = lax.rem(lax.div(sequence, y_size), x_size)
    z_high = lax.div(sequence, y_size * x_size)
    z_place = z_high * dp_size + sample
    z_stride = GROUP * y_size * x_size
    rounds = [
        (
            z_place,
            z_size * dp_size,
            z_slots,
            lambda p: {
                "seq": position + (lax.div(p, dp_size) - z_high) * z_stride,
                "dp": lax.rem(p, dp_size),
            },
        ),
        (
            x_place,
            x_size,
            x_slots,
            lambda p: {"seq": position + (p - x_place) * GROUP * y_size},
        ),
        (ring_place, GROUP * y_size, y_slots, lambda p: {"seq": ring_base + p}),
    ]

    def rows_of(which):
        return pl.ds(pl.multiple_of(which * rows, 16), rows)

    def columns_of(which, head):
        return pl.ds(pl.multiple_of((which * heads + head) * HD, HD), HD)

    def remote(src, dst, send_sem, recv_sem, device):
        return pltpu.make_async_remote_copy(
            src_ref=src,
            dst_ref=dst,
            send_sem=send_sem,
            recv_sem=recv_sem,
            device_id=device,
            device_id_type=MESH,
        )

    def in_pair(head, k):
        theirs = columns_of(partners[k], head)
        mine = rows_of(member)
        ends = (
            (qkv.at[0, :, 0, :, theirs], held.at[head, pl.ds(0, 3), mine, :]),
            (cot.at[0, 0, :, theirs], held.at[head, 3, mine, :]),
        )
        if k == 0:
            return [
                pltpu.make_async_copy(src, dst, in_recv.at[head, k, t])
                for t, (src, dst) in enumerate(ends)
            ]
        return [
            remote(
                src,
                dst,
                in_send.at[head, k, t],
                in_recv.at[head, k, t],
                {"seq": base + partners[k]},
            )
            for t, (src, dst) in enumerate(ends)
        ]

    def in_arrival(head, k):
        theirs = rows_of(partners[k])
        return [
            remote(
                dst,
                dst,
                in_send.at[head, k, t],
                in_recv.at[head, k, t],
                {"seq": base + partners[k]},
            )
            for t, dst in enumerate(
                (held.at[head, pl.ds(0, 3), theirs, :], held.at[head, 3, theirs, :])
            )
        ]

    def out_pair(head, k, t):
        theirs = rows_of(partners[k])
        mine = columns_of(member, head)
        if t == 0:
            src, dst = made.at[head, 0, theirs, :], blended.at[0, 0, :, mine]
        else:
            src, dst = made.at[head, pl.ds(1, 3), theirs, :], grads.at[0, :, 0, :, mine]
        if k == 0:
            return pltpu.make_async_copy(src, dst, out_recv.at[head, k, t])
        return remote(
            src,
            dst,
            out_send.at[head, k, t],
            out_recv.at[head, k, t],
            {"seq": base + partners[k]},
        )

    def out_arrival(head, k, t):
        theirs = columns_of(partners[k], head)
        dst = blended.at[0, 0, :, theirs] if t == 0 else grads.at[0, :, 0, :, theirs]
        return remote(
            dst,
            dst,
            out_send.at[head, k, t],
            out_recv.at[head, k, t],
            {"seq": base + partners[k]},
        )

    def back_copy(head):
        return remote(
            back_out.at[head],
            back_in.at[head],
            back_sems.at[head, 0],
            back_sems.at[head, 1],
            other_core,
        )

    def res_copy(head):
        return remote(
            res_out.at[head],
            res_in.at[head],
            res_sems.at[head, 0],
            res_sems.at[head, 1],
            other_core,
        )

    total_copy = remote(total, total, total_sems.at[0], total_sems.at[1], other_core)

    def round_copies(which):
        place, number, slots, device = rounds[which]
        return [
            remote(
                slots.at[place],
                slots.at[place],
                round_send.at[which, ahead],
                round_recv.at[which, ahead],
                device(lax.rem(place + ahead, number)),
            )
            for ahead in range(1, number)
        ]

    def round_start(which, mine):
        place, _, slots, _ = rounds[which]
        slots[place] = mine
        for copy in round_copies(which):
            copy.start()

    def round_finish(which):
        place, number, slots, device = rounds[which]
        for ahead in range(1, number):
            sender = lax.rem(place + number - ahead, number)
            remote(
                slots.at[sender],
                slots.at[sender],
                round_send.at[which, ahead],
                round_recv.at[which, ahead],
                device(sender),
            ).wait_recv()
        for copy in round_copies(which):
            copy.wait_send()

    def slot_sum(which):
        _, number, slots, _ = rounds[which]
        added = slots[0]
        for slot in range(1, number):
            added = added + slots[slot]
        return added

    small = [
        pltpu.make_async_copy(src, dst, small_sems.at[i])
        for i, (src, dst) in enumerate(
            ((tile_map, order_all), (gate, gains_all), (text_count, counts))
        )
    ]
    for copy in small:
        copy.start()
    for head in range(heads):
        for copy in in_pair(head, 0):
            copy.start()

    barrier = pltpu.get_barrier_semaphore()

    def greet(peer, semaphore=barrier):
        pl.semaphore_signal(semaphore, inc=1, device_id=peer, device_id_type=MESH)

    def greet_partner(k, semaphore=barrier):
        greet({"seq": base + partners[k]}, semaphore)

    @pl.when(core == 0)
    def _():
        far = []
        for place, number, _, device in rounds[:2]:
            far += [device(lax.rem(place + ahead, number)) for ahead in range(1, number)]
        if y_size == 2:
            far += [{"seq": ring_base + (1 - y_place) * GROUP + k} for k in range(GROUP)]
        for k in (1, 2, 3):
            greet_partner(k)
        for peer in far:
            greet(peer)
        pl.semaphore_wait(barrier, GROUP + len(far))
        greet(other_core, entered)
        for head in range(heads - 1):
            for k in (2, 3, 1):
                for copy in in_pair(head, k):
                    copy.start()

    @pl.when(core == 1)
    def _():
        greet_partner(2)
        greet(other_core)

        @pl.when(member == 0)
        def _():
            greet_partner(1)

        @pl.when(member == 1)
        def _():
            pl.semaphore_wait(barrier, 2)

        @pl.when(member != 1)
        def _():
            pl.semaphore_wait(barrier, 1)

        for head in range(heads - 1):
            for copy in in_pair(head, 2):
                copy.start()

        @pl.when(member == 1)
        def _():
            greet_partner(1, known)
            pl.semaphore_wait(known, 1)
            greet_partner(2, known)

        @pl.when(member == 0)
        def _():
            pl.semaphore_wait(known, 1)
            greet_partner(1, known)
            greet_partner(2, known)

        @pl.when(member >= 2)
        def _():
            pl.semaphore_wait(known, 1)

        for head in range(heads - 1):
            for k in (3, 1):
                for copy in in_pair(head, k):
                    copy.start()

    for copy in small:
        copy.wait()
    partial[...] = jnp.zeros(partial.shape, F32)
    counted = counts[0, sequence]

    @pl.when(core == 1)
    def _():
        order = order_all[0, pl.ds(sequence, 1), :].astype(F32)
        down = lax.broadcasted_iota(jnp.int32, (length, length), 0).astype(F32)
        perm_t[...] = jnp.where(down == order, 1.0, 0.0).astype(BF16)
        order_down = jnp.transpose(jnp.broadcast_to(order, (HD, length)))
        for start in range(0, length, HD):
            width = min(HD, length - start)
            across = lax.broadcasted_iota(jnp.int32, (length, width), 1).astype(F32) + start
            perm[:, start : start + width] = jnp.where(
                order_down[:, :width] == across, 1.0, 0.0
            ).astype(BF16)

    for k in (2, 3, 1):
        for copy in in_pair(0, k):
            copy.wait_send()
    for k in (2, 3, 1):
        for copy in in_pair(heads - 1, k):
            copy.start()

    def arrive(head):
        for k in range(GROUP):
            for copy in in_pair(head, k) if k == 0 else in_arrival(head, k):
                if k == 0:
                    copy.wait()
                else:
                    copy.wait_recv()

        @pl.when(core == 1)
        def _():
            back_out[head] = contract(perm[...], held[head, 3], 1, 0).astype(BF16)
            back_copy(head).start()

    def depart(head):
        for k in (2, 3, 1, 0):
            out_pair(head, k, 1).start()

        @pl.when(core == 1)
        def _():
            res_copy(head).wait_recv()
            placed = contract(perm_t[...], res_in[head], 1, 0)
            made[head, 0] = (made[head, 0].astype(F32) + placed).astype(BF16)

        for k in (2, 3, 1, 0):
            out_pair(head, k, 0).start()

    @pl.when(core == 1)
    def _():
        pl.semaphore_wait(entered, 1)

    for head in range(heads - 1):
        arrive(head)

    blocks = [(start, min(BLOCK, length - start)) for start in range(0, length, BLOCK)]

    def one_head(head, carry):
        @pl.when(head == heads - 1)
        def _():
            arrive(head)

        gains = gains_all[pl.ds(member * heads + head, 1), :]
        keys = held[head, 1]
        values = held[head, 2]
        for start, width in blocks:
            span = pl.ds(start, width)
            scores = contract(keys, held[head, 0, span, :], 1, 1)
            text = lax.broadcasted_iota(jnp.int32, (TXT, width), 0) < counted
            scores = jnp.concatenate(
                [jnp.where(text, scores[:TXT], -jnp.inf), scores[TXT:]], axis=0
            )
            top = jnp.max(scores, axis=0, keepdims=True)
            grown = jnp.exp2((scores - top) * EXP2_SCALE)
            probs = grown * (1.0 / jnp.sum(grown, axis=0, keepdims=True))
            probs_low = probs.astype(BF16)
            probs_all[:, start : start + width] = probs
            probs_low_all[:, start : start + width] = probs_low
            made[head, 0, span, :] = jnp.transpose(contract(values, probs_low, 0, 0)).astype(BF16)

        @pl.when(core == 0)
        def _():
            own = made[head, 0].astype(F32)
            res_out[head] = (gains * own).astype(BF16)
            res_copy(head).start()
            back_copy(head).wait_recv()
            back = back_in[head].astype(F32)
            partial[pl.ds(head, 1), :] = jnp.sum(own * back, axis=0, keepdims=True)
            held[head, 3] = (held[head, 3].astype(F32) + gains * back).astype(BF16)

            @pl.when(head == heads - 1)
            def _():
                round_start(0, partial[...])
                round_finish(0)
                round_start(1, slot_sum(0))
                round_finish(1)
                round_start(2, slot_sum(1))

        key_sum = value_sum = None
        for start, width in blocks:
            span = pl.ds(start, width)
            queries = held[head, 0, span, :]
            grad = held[head, 3, span, :]
            probs = probs_all[:, start : start + width]
            grad_probs = contract(values, grad, 1, 1)
            centre = jnp.sum(probs * grad_probs, axis=0, keepdims=True)
            shifted = (probs * (grad_probs - centre)).astype(BF16)
            made[head, 1, span, :] = (
                jnp.transpose(contract(keys, shifted, 0, 0)) * SCALE
            ).astype(BF16)
            key_part = contract(shifted, queries, 1, 0)
            value_part = contract(probs_low_all[:, start : start + width], grad, 1, 0)
            key_sum = key_part if key_sum is None else key_sum + key_part
            value_sum = value_part if value_sum is None else value_sum + value_part
        made[head, 2] = (key_sum * SCALE).astype(BF16)
        made[head, 3] = value_sum.astype(BF16)

        @pl.when(head == heads - 2)
        def _():
            for later in range(1, heads):
                for k in (2, 3, 1):
                    for copy in in_pair(later, k):
                        copy.wait_send()
            for earlier in range(heads - 1):
                depart(earlier)

        @pl.when(head == heads - 1)
        def _():
            depart(head)

        return carry

    lax.fori_loop(0, heads, one_head, 0)

    @pl.when(core == 0)
    def _():
        round_finish(2)
        for which in range(GROUP):
            added = y_slots[which, :heads, :]
            for half in range(1, y_size):
                added = added + y_slots[half * GROUP + which, :heads, :]
            total[which * heads : (which + 1) * heads, :] = added
        total_copy.start()
        total_copy.wait_send()

    @pl.when(core == 1)
    def _():
        total_copy.wait_recv()

    gate_grad[...] = total[...]

    def finish(head, carry):
        for t in (0, 1):
            out_pair(head, 0, t).wait()
            for k in (1, 2, 3):
                out_pair(head, k, t).wait_send()
                out_arrival(head, k, t).wait_recv()

        @pl.when(core == 0)
        def _():
            res_copy(head).wait_send()

        @pl.when(core == 1)
        def _():
            back_copy(head).wait_send()

        return carry

    lax.fori_loop(0, heads, finish, 0)


def store(*refs):
    sems = refs[-1]
    number = len(refs) // 2
    copies = [
        pltpu.make_async_copy(refs[i], refs[number + i], sems.at[i]) for i in range(number)
    ]
    for copy in copies:
        copy.start()
    for copy in copies:
        copy.wait()


def per_device(mesh, qkv, cotangent, gate, tile_map, text_count):
    rows, channels = qkv.shape[3:]
    length = rows * GROUP
    heads = channels // HD // GROUP
    groups = mesh.shape["seq"] // GROUP
    dp_size = mesh.shape["dp"]
    y_size = min(2, groups)
    x_size = min(4, groups // y_size)
    z_size = groups // (y_size * x_size)
    places = max(z_size * dp_size, x_size, GROUP * y_size)
    vmem = pl.BlockSpec(memory_space=pltpu.VMEM)
    hbm = pl.BlockSpec(memory_space=pltpu.HBM)
    any_space = pl.BlockSpec(memory_space=pl.ANY)
    dma = pltpu.SemaphoreType.DMA
    blended, grads, gate_grad = pl.pallas_call(
        functools.partial(kernel, heads, (z_size, dp_size, x_size, y_size)),
        out_shape=(
            pltpu.VMEM(cotangent.shape, BF16),
            pltpu.VMEM(qkv.shape, BF16),
            pltpu.VMEM((channels // HD, HD), F32),
        ),
        in_specs=[hbm] * 5,
        out_specs=(any_space, any_space, vmem),
        scratch_shapes=[
            pltpu.VMEM((heads, 4, length, HD), BF16),
            pltpu.VMEM((heads, 4, length, HD), BF16),
            pltpu.VMEM((heads, length, HD), BF16),
            pltpu.VMEM((heads, length, HD), BF16),
            pltpu.VMEM((heads, length, HD), BF16),
            pltpu.VMEM((heads, length, HD), BF16),
            pltpu.VMEM((length, length), BF16),
            pltpu.VMEM((length, length), BF16),
            pltpu.VMEM((length, length), F32),
            pltpu.VMEM((length, length), BF16),
            pltpu.VMEM(tile_map.shape, jnp.int32),
            pltpu.VMEM((channels // HD, HD), F32),
            pltpu.SMEM(text_count.shape, jnp.int32),
            pltpu.VMEM((8, HD), F32),
            pltpu.VMEM((z_size * dp_size, 8, HD), F32),
            pltpu.VMEM((x_size, 8, HD), F32),
            pltpu.VMEM((GROUP * y_size, 8, HD), F32),
            pltpu.VMEM((channels // HD, HD), F32),
            dma((heads, GROUP, 2)),
            dma((heads, GROUP, 2)),
            dma((heads, GROUP, 2)),
            dma((heads, GROUP, 2)),
            dma((heads, 2)),
            dma((heads, 2)),
            dma((3, places)),
            dma((3, places)),
            dma((2,)),
            dma((3,)),
            pltpu.SemaphoreType.REGULAR,
            pltpu.SemaphoreType.REGULAR,
        ],
        compiler_params=pltpu.CompilerParams(
            collective_id=0, has_side_effects=True, vmem_limit_bytes=44 * 1024 * 1024
        ),
    )(
        *(
            pltpu.with_memory_space_constraint(operand, pltpu.HBM)
            for operand in (qkv, cotangent, gate.reshape(channels // HD, HD), tile_map, text_count)
        )
    )
    results = (blended, grads, gate_grad.reshape(channels))
    return pl.pallas_call(
        store,
        out_shape=tuple(pltpu.HBM(result.shape, result.dtype) for result in results),
        in_specs=[any_space] * 3,
        out_specs=(any_space,) * 3,
        scratch_shapes=[dma((3,))],
    )(*(pltpu.with_memory_space_constraint(result, pltpu.VMEM) for result in results))


def solution(mesh):
    placed = (
        P("grp", None, "dp", "seq", None),
        P("grp", "dp", "seq", None),
        P(),
        P("dp", None, None),
        P("dp", None),
    )
    return jax.shard_map(
        functools.partial(per_device, mesh),
        mesh=mesh,
        in_specs=placed,
        out_specs=(P("grp", "dp", "seq", None), P("grp", None, "dp", "seq", None), P()),
        check_vma=False,
    )
```
